256 devices in a mesh: frame: 8 (over y, core), space: 32 (over z, x).
Axes of the slice: x: 4, y: 4, z: 8, core: 2. Of those that a mesh axis runs over, the one named last changes fastest.
Arguments:
- latents: bfloat16 [8, 64, 64, 768], P('frame', 'space'), may hold values from -6 to 6
- occupancy: int32 [64, 64], P('space'), may hold values 0 or 1
- neighbors: int32 [64, 6], P('space'), may hold values from -1 to 63, as said below
- brick_counts: int32 [64], replicated, may hold values from 1 to 64, as said below
- noise_levels: int32 [8], P('frame'), may hold values from 0 to 15
- level_embed: float32 [16, 768], replicated, may hold values from -6 to 6
- occupied_embed: float32 [768], replicated, may hold values from -6 to 6
- step_size: float32 [16], replicated, may hold values from 0.25 to 1
- fresh_noise: bfloat16 [64, 64, 768], P('space'), may hold values from -6 to 6
- space_project: bfloat16 [768, 2304], replicated, may hold values from -2 to 2
- space_output: bfloat16 [768, 768], replicated, may hold values from -0.21875 to 0.21875
- time_project: bfloat16 [768, 2304], replicated, may hold values from -2 to 2
- time_output: bfloat16 [768, 768], replicated, may hold values from -0.21875 to 0.21875
- expand_weight: bfloat16 [768, 1536], P(None, 'space'), may hold values from -0.21875 to 0.21875
- reduce_weight: bfloat16 [1536, 768], P('space'), may hold values from -0.15625 to 0.15625
Outputs:
- generated: bfloat16 [8, 64, 64, 768], P('frame', 'space')
The draws below stay inside these ranges and needn't reach their ends.
Inputs may be any that keep to these rules, and one draw needn't show every extreme that they name: `neighbors`: each entry is -1 (no brick there) or the index of another brick of the same frame whose index differs from the row's own by 1 to 2; a difference of exactly 2 occurs in every draw. `brick_counts`: the valid tokens of a brick are its first ones; some brick is full.
All inputs are finite; a program needn't handle non-finite values. No bound on the sum of `occupancy` on one device may be relied on, other than what follows from the above.
Results may differ from the reference program's by a relative error of at most 0.02.
Values may be sent and summed in bfloat16 or wider, within the bound.
No kernel may reach another device: no remote copies, remote signals or barrier semaphores. Data moves between devices by JAX's collectives and lax.ppermute only.
A program may use at most 128 MiB of HBM per device.

```python
import math
import jax
import jax.numpy as jnp
from jax import lax

D = 768
HEADS = 12
HD = 64
MLPH = 1536
BRICK = 64
LEVELS = 16
B_DEV = 2
FRAMES = 8
NB = 64


def drawn_projection(key, strength):
    key_parts = jax.random.split(key, 4)
    base_part = jax.random.normal(key_parts[0], (D, 3 * D), jnp.float32) * D ** (-0.5)
    direction = jax.random.normal(key_parts[1], (D,), jnp.float32) * D ** (-0.5)
    pattern = jax.random.normal(key_parts[2], (HEADS, HD), jnp.float32)
    levels = jax.random.uniform(key_parts[3], (HEADS, 1), jnp.float32, 0.5, 1.5) * strength
    shared = (levels * pattern).reshape(D)
    extra_part = direction[:, None] * shared[None, :]
    zero_block = jnp.zeros((D, D), jnp.float32)
    added_part = jnp.concatenate([extra_part, extra_part, zero_block], axis=1)
    return jnp.clip(base_part + added_part, -2.0, 2.0)


def draw_space_project(key, part):
    key = jax.random.fold_in(key, 21)
    return drawn_projection(key, 0.0).astype(jnp.bfloat16)


def draw_time_project(key, part):
    key = jax.random.fold_in(key, 22)
    return drawn_projection(key, 0.0).astype(jnp.bfloat16)


def draw_brick_counts(key, part):
    key = jax.random.fold_in(key, 11)
    key_parts = jax.random.split(key, 2)
    filled = jax.random.randint(key_parts[0], (NB,), 1, BRICK + 1)
    chosen = jax.random.randint(key_parts[1], (), 0, NB)
    return jnp.where(jnp.arange(NB) == chosen, BRICK, filled).astype(jnp.int32)


def draw_neighbors(key, part):
    key = jax.random.fold_in(key, 12)
    key_parts = jax.random.split(key, 2)
    reach_size = jax.random.randint(key_parts[0], (NB, 6), 1, B_DEV + 1)
    missing = jax.random.randint(key_parts[1], (NB, 6), 0, 4) == 0
    direction_sign = jnp.where(jnp.arange(6) % 2 == 0, 1, -1)
    own_index = jnp.arange(NB, dtype=jnp.int32)[:, None]
    target = own_index + direction_sign[None, :] * reach_size
    kept_mask = jnp.logical_not(missing) & (target >= 0) & (target < NB)
    chosen = NB - 1 - B_DEV
    forced = (own_index == chosen) & (jnp.arange(6)[None, :] == 0)
    target = jnp.where(forced, NB - 1, target)
    kept_mask = kept_mask | forced
    return jnp.where(kept_mask, target, -1).astype(jnp.int32)


def plant(entries, own_key, low, largest):
    shape = entries.shape
    index_at = [jax.random.randint(jax.random.fold_in(own_key, axis), (), 0, shape[axis]) for axis in range(len(shape))]
    entries = entries.at[tuple(index_at)].set(low)
    longest = shape.index(max(shape))
    index_at[longest] = (index_at[longest] + 1) % shape[longest]
    return entries.at[tuple(index_at)].set(largest)


def steps_of(key, shape, cuts, smallest, largest):
    def one(axis_at, blocks):
        draws = jax.random.uniform(jax.random.fold_in(jax.random.fold_in(key, 6), axis_at), (blocks,), jnp.float32, smallest / len(cuts), largest / len(cuts))
        return jnp.repeat(jnp.exp(draws), shape[axis_at] // blocks).reshape((-1,) + (1,) * (len(shape) - axis_at - 1))

    loudness = one(*cuts[0])
    for cut in cuts[1:]:
        loudness = loudness * one(*cut)
    return loudness


def normal_values(own_key, extent, spread, reach, pieces=(), kind=jnp.bfloat16):
    entries = jax.random.normal(own_key, extent, jnp.float32) * spread
    if len(pieces) > 0:
        entries = steps_of(own_key, extent, pieces, -0.22, 0.18) * entries
    return jnp.clip(entries, min=-reach, max=reach).astype(kind)


def setup_inputs(seed: int = 0) -> dict:
    key_list = jax.random.split(jax.random.key(seed), 16)
    return {
        "latents": normal_values(key_list[0], (FRAMES, NB, BRICK, D), 1.0, 6.0, ((0, 8), (1, 32))),
        "occupancy": plant((jax.random.randint(key_list[1], (NB, BRICK), 0, 2) < 1).astype(jnp.int32), jax.random.fold_in(key_list[1], 1), 0, 1),
        "neighbors": draw_neighbors(jax.random.fold_in(key_list[15], 71), 0),
        "brick_counts": draw_brick_counts(jax.random.fold_in(key_list[15], 71), 0),
        "noise_levels": plant(jax.random.randint(key_list[4], (FRAMES,), 0, LEVELS), jax.random.fold_in(key_list[4], 1), 0, LEVELS - 1).astype(jnp.int32),
        "level_embed": normal_values(key_list[5], (LEVELS, D), 1.0, 6.0, (), jnp.float32),
        "occupied_embed": normal_values(key_list[6], (D,), 1.0, 6.0, (), jnp.float32),
        "step_size": jnp.clip(jnp.exp(jax.random.uniform(key_list[7], (LEVELS,), jnp.float32, math.log(0.25), math.log(1.0))), 0.25, 1.0),
        "fresh_noise": normal_values(key_list[8], (NB, BRICK, D), 1.0, 6.0, ((0, 32),)),
        "space_project": draw_space_project(jax.random.fold_in(key_list[15], 71), 0),
        "space_output": normal_values(key_list[10], (D, D), D ** -0.5, 0.21875),
        "time_project": draw_time_project(jax.random.fold_in(key_list[15], 71), 0),
        "time_output": normal_values(key_list[12], (D, D), D ** -0.5, 0.21875),
        "expand_weight": normal_values(key_list[13], (D, MLPH), D ** -0.5, 0.21875, ((1, 32),)),
        "reduce_weight": normal_values(key_list[14], (MLPH, D), MLPH ** -0.5, 0.15625, ((0, 32),)),
    }


epsilon = 1e-06
masked_score = -1e+30

def rms_norm(values):
    return values * lax.rsqrt(lax.optimization_barrier(jnp.mean(values * values, axis=-1, keepdims=True)) + epsilon)

def window_attend(queries, key_rows, value_rows, usable, heads):
    blocks, query_count, model_width = queries.shape
    head_size = model_width // heads
    query_heads = queries.reshape(blocks, query_count, heads, head_size).astype(jnp.float32)
    key_heads = key_rows.reshape(blocks, -1, heads, head_size).astype(jnp.float32)
    value_heads = value_rows.reshape(blocks, -1, heads, head_size).astype(jnp.float32)
    scores = jnp.einsum('bqhd,bkhd->bhqk', query_heads, key_heads) / math.sqrt(head_size)
    scores = jnp.where(usable, scores, masked_score)
    highest = lax.optimization_barrier(jnp.max(scores, axis=-1, keepdims=True))
    raised = jnp.where(usable, jnp.exp(scores - highest), 0.0)
    weights = (raised / lax.optimization_barrier(jnp.sum(raised, axis=-1, keepdims=True))).astype(jnp.bfloat16)
    mixture = jnp.einsum('bhqk,bkhd->bqhd', weights.astype(jnp.float32), value_heads)
    return mixture.astype(jnp.bfloat16).reshape(blocks, query_count, model_width)

def denoise(state, occupancy, neighbors, brick_counts, noise_levels, level_embed, occupied_embed, step_size, space_project, space_output, time_project, time_output, expand_weight, reduce_weight):
    frame_count, brick_total, brick_size, model_width = state.shape
    token_count = brick_total * brick_size
    head_size = model_width // HEADS
    level_rows = level_embed[noise_levels]
    strides = step_size[noise_levels]
    before = state.astype(jnp.float32) + occupancy[None, :, :, None].astype(jnp.float32) * occupied_embed
    before = before + level_rows[:, None, None, :]
    normed = rms_norm(before).astype(jnp.bfloat16)
    flat_rows = normed.reshape(frame_count * token_count, model_width)
    space_triple = jnp.dot(flat_rows, space_project, preferred_element_type=jnp.float32).astype(jnp.bfloat16)
    space_triple = space_triple.reshape(frame_count, brick_total, brick_size, 3 * model_width)
    own_bricks = jnp.arange(brick_total, dtype=jnp.int32)[:, None]
    key_bricks = jnp.concatenate([own_bricks, jnp.maximum(neighbors, 0)], axis=1).astype(jnp.int32)
    present = jnp.concatenate([jnp.ones((brick_total, 1), dtype=bool), neighbors >= 0], axis=1)
    key_counts = brick_counts[key_bricks]
    slot_index = jnp.arange(brick_size, dtype=jnp.int32)
    usable = (present[..., None] & (slot_index < key_counts[..., None])).reshape(brick_total, 1, 1, 7 * brick_size)

    def one_frame(frame_triple):
        queries = frame_triple[..., :model_width]
        gathered = frame_triple[:, :, model_width:][key_bricks]
        gathered = gathered.reshape(brick_total, 7 * brick_size, 2 * model_width)
        return window_attend(queries, gathered[..., :model_width], gathered[..., model_width:], usable, HEADS)
    space_mix = lax.map(one_frame, space_triple)
    space_term = jnp.dot(space_mix.reshape(-1, model_width), space_output, preferred_element_type=jnp.float32)
    time_triple = jnp.dot(flat_rows, time_project, preferred_element_type=jnp.float32).astype(jnp.bfloat16)
    time_triple = time_triple.reshape(frame_count, token_count, 3 * model_width)
    queries = time_triple[..., :model_width].astype(jnp.float32).reshape(frame_count, token_count, HEADS, head_size)
    key_heads = time_triple[..., model_width:2 * model_width].astype(jnp.float32).reshape(frame_count, token_count, HEADS, head_size)
    value_heads = time_triple[..., 2 * model_width:].astype(jnp.float32).reshape(frame_count, token_count, HEADS, head_size)
    scores = jnp.einsum('fnhd,gnhd->nhfg', queries, key_heads) / math.sqrt(head_size)
    causal = jnp.arange(frame_count)[:, None] >= jnp.arange(frame_count)[None, :]
    scores = jnp.where(causal, scores, masked_score)
    highest = lax.optimization_barrier(jnp.max(scores, axis=-1, keepdims=True))
    raised = jnp.where(causal, jnp.exp(scores - highest), 0.0)
    weights = raised / lax.optimization_barrier(jnp.sum(raised, axis=-1, keepdims=True))
    time_mix = jnp.einsum('nhfg,gnhd->fnhd', weights, value_heads).astype(jnp.bfloat16)
    time_mix = time_mix.reshape(frame_count * token_count, model_width)
    time_term = jnp.dot(time_mix, time_output, preferred_element_type=jnp.float32)
    middle = before.reshape(-1, model_width) + space_term + time_term
    middle_normed = rms_norm(middle).astype(jnp.bfloat16)
    hidden = jax.nn.gelu(jnp.dot(middle_normed, expand_weight, preferred_element_type=jnp.float32), approximate=True)
    hidden = hidden.astype(jnp.bfloat16)
    feed_term = jnp.dot(hidden, reduce_weight, preferred_element_type=jnp.float32)
    change = space_term + time_term + feed_term
    moved = state.reshape(-1, model_width).astype(jnp.float32) + jnp.repeat(strides, token_count)[:, None] * change
    return moved.astype(jnp.bfloat16).reshape(state.shape)

def reference(latents, occupancy, neighbors, brick_counts, noise_levels, level_embed, occupied_embed, step_size, fresh_noise, space_project, space_output, time_project, time_output, expand_weight, reduce_weight):
    first = denoise(latents, occupancy, neighbors, brick_counts, noise_levels, level_embed, occupied_embed, step_size, space_project, space_output, time_project, time_output, expand_weight, reduce_weight)
    window = jnp.concatenate([first[1:], fresh_noise[None]], axis=0)
    return denoise(window, occupancy, neighbors, brick_counts, noise_levels, level_embed, occupied_embed, step_size, space_project, space_output, time_project, time_output, expand_weight, reduce_weight)
```

```python
import jax
import jax.numpy as jnp
from jax import lax
from jax.experimental import pallas as pl
from jax.experimental.pallas import tpu as pltpu
from jax.sharding import PartitionSpec as P

HEADS = 12
FRAMES = 8
YS = 4
EPSILON = 1e-06
MASKED = -1e30

F32 = jnp.float32
BF16 = jnp.bfloat16
VMEM_LIMIT = 40 * 1024 * 1024

I_FRAME, I_SPACE, I_Y, I_CORE, I_LEVEL, I_NEXT_LEVEL = range(6)

vmem = pl.BlockSpec(memory_space=pltpu.VMEM)
smem = pl.BlockSpec(memory_space=pltpu.SMEM)
anywhere = pl.BlockSpec(memory_space=pl.ANY)


def dot(a, b):
    return jnp.dot(a, b, preferred_element_type=F32)


def dot_t(a, b):
    return lax.dot_general(a, b, (((1,), (1,)), ((), ())), preferred_element_type=F32)


def rms(values):
    return values * lax.rsqrt(jnp.mean(values * values, axis=-1, keepdims=True) + EPSILON)


def chunk_rows(index, rows):
    return pl.ds(pl.multiple_of(index * rows, rows), rows)


def call(kernel, outs, specs, scratch=(), flops=0, moved=0):
    return pl.pallas_call(
        kernel,
        out_shape=outs,
        in_specs=specs,
        out_specs=jax.tree.map(lambda _: vmem, outs),
        scratch_shapes=scratch,
        compiler_params=pltpu.CompilerParams(vmem_limit_bytes=VMEM_LIMIT),
        cost_estimate=pl.CostEstimate(flops=flops, bytes_accessed=moved, transcendentals=0),
    )


def state_before(state, occupied, embed, level):
    return state.astype(F32) + occupied * embed + level


def pre_kernel(info, state, occupied, embed, levels, normed, *chunks):
    level = levels[pl.ds(info[I_LEVEL], 1), :]
    before = state_before(state[...], occupied[...], embed[...], level)
    normed[...] = rms(before).astype(BF16)
    send_chunks(info, normed, chunks)


def send_chunks(info, rows, chunks):
    size = rows.shape[0] // YS
    for k, chunk in enumerate(chunks):
        chunk[...] = rows[chunk_rows(lax.rem(info[I_Y] + k, YS), size), :]


def time_project_kernel(shift, info, c0, c1, c2, c3, project, queries, pairs, rows):
    size = c0.shape[0]
    for k, chunk in enumerate((c0, c1, c2, c3)):
        at = lax.rem(info[I_Y] + YS - k + shift * (YS - info[I_CORE]), YS)
        rows[chunk_rows(at, size), :] = chunk[...]
    width = rows.shape[1]
    values = rows[...]
    pairs[...] = dot(values, project[:, width:]).astype(BF16)
    queries[...] = dot(values, project[:, :width]).astype(BF16)


def head_selector(width):
    lane = lax.broadcasted_iota(jnp.int32, (width, 128), 0)
    head = lax.broadcasted_iota(jnp.int32, (width, 128), 1)
    return (lane // (width // HEADS) == head).astype(BF16)


def head_spreader(width):
    head = lax.broadcasted_iota(jnp.int32, (128, width), 0)
    lane = lax.broadcasted_iota(jnp.int32, (128, width), 1)
    return (lane // (width // HEADS) == head).astype(BF16)


def time_attend_kernel(info, queries, mine, other, m0, m1, m2, m3, mixed):
    tokens = queries.shape[0] // YS
    width = queries.shape[1]
    scale = (width // HEADS) ** -0.5
    selector = head_selector(width)
    first_core = info[I_CORE] == 0
    scores = {}
    for side, pairs in enumerate((mine, other)):
        for i in range(YS):
            left = YS - i
            keys = pairs[i * tokens : (i + 1) * tokens, :width].astype(F32)
            query = queries[i * tokens :, :].astype(F32).reshape(left, tokens, width)
            product = (query * keys[None]).reshape(left * tokens, width)
            high = product.astype(BF16)
            low = (product - high.astype(F32)).astype(BF16)
            score = (dot(high, selector) + dot(low, selector)) * scale
            for j in range(i, YS):
                part = score[(j - i) * tokens : (j - i + 1) * tokens, :]
                if side == 1 and i == j:
                    part = jnp.where(first_core, MASKED, part)
                scores[side, i, j] = part
    weights = []
    for j in range(YS):
        parts = [scores[side, i, j] for side in range(2) for i in range(j + 1)]
        highest = parts[0]
        for part in parts[1:]:
            highest = jnp.maximum(highest, part)
        raised = [jnp.exp(part - highest) for part in parts]
        total = raised[0]
        for part in raised[1:]:
            total = total + part
        weights += [(part / total).astype(BF16) for part in raised]
    spread = dot(jnp.concatenate(weights, axis=0), head_spreader(width))
    at = 0
    for j in range(YS):
        mix = None
        for pairs in (mine, other):
            for i in range(j + 1):
                value = pairs[i * tokens : (i + 1) * tokens, width:].astype(F32)
                term = spread[at * tokens : (at + 1) * tokens, :] * value
                mix = term if mix is None else mix + term
                at += 1
        mixed[j * tokens : (j + 1) * tokens, :] = mix.astype(BF16)
    send_chunks(info, mixed, (m0, m1, m2, m3))


def space_project_kernel(info, state, occupied, embed, levels, left, right, project, queries, pairs):
    width = state.shape[1]
    count = state.shape[0]
    level = levels[pl.ds(info[I_LEVEL], 1), :]
    before = state_before(state[...], occupied[...], embed[...], level)
    own = rms(before).astype(BF16)
    scale = (width // HEADS) ** -0.5
    queries[...] = (dot(own, project[:, :width]).astype(BF16) * scale).astype(BF16)
    pairs[count : 2 * count, :] = dot(own, project[:, width:]).astype(BF16)
    pairs[:count, :] = dot(left[...], project[:, width:]).astype(BF16)
    pairs[2 * count :, :] = dot(right[...], project[:, width:]).astype(BF16)


def space_attend_kernel(info, neighbors, counts, queries, pairs, output, term, mixed):
    rows, width = queries.shape
    blocks = neighbors.shape[0]
    brick = rows // blocks
    keys = pairs.shape[0]
    nearby = keys // brick
    total_bricks = counts.shape[0]
    column = lax.broadcasted_iota(jnp.int32, (1, keys), 1)
    key_brick = column // brick
    slot = column % brick
    times = []
    for b in range(blocks):
        row = jnp.zeros((1, keys), F32)
        for e in range(nearby):
            index = (info[I_SPACE] - 1) * blocks + e
            inside = (index >= 0) & (index < total_bricks)
            number = jnp.int32(1 if e == blocks + b else 0)
            for n in range(neighbors.shape[1]):
                number = number + jnp.where(inside & (neighbors[b, n] == index), 1, 0)
            valid = counts[jnp.clip(index, 0, total_bricks - 1)]
            row = jnp.where((key_brick == e) & (slot < valid), number.astype(F32), row)
        times.append(jnp.broadcast_to(row, (brick, keys)))
    times = jnp.concatenate(times + times, axis=0)
    usable = times > 0.0
    pair = 2 * (width // HEADS)
    half = lax.broadcasted_iota(jnp.int32, (rows, pair), 1) < pair // 2
    for h in range(HEADS // 2):
        lanes = slice(h * pair, (h + 1) * pair)
        query = queries[:, lanes]
        zero = jnp.zeros_like(query)
        both = jnp.concatenate([jnp.where(half, query, zero), jnp.where(half, zero, query)], axis=0)
        score = jnp.where(usable, dot_t(both, pairs[:, lanes]), MASKED)
        highest = jnp.max(score, axis=-1, keepdims=True)
        raised = jnp.exp(score - highest) * times
        share = (raised / jnp.sum(raised, axis=-1, keepdims=True)).astype(BF16)
        mix = dot(share, pairs[:, width + h * pair : width + (h + 1) * pair])
        mixed[:, lanes] = jnp.where(half, mix[:rows], mix[rows:]).astype(BF16)
    term[...] = dot(mixed[...], output[...])


def finish_kernel(
    hand_on, info, steps, state, occupied, embed, levels, space_term, m0, m1, m2, m3, output, *rest
):
    weights = rest[:8]
    if hand_on:
        fresh, moved, normed = rest[8:11]
        chunks = rest[11:15]
        expand, reduce, mixed, sems = rest[15:]
    else:
        moved = rest[8]
        expand, reduce, mixed, sems = rest[9:]
    parts = len(weights) // 2
    deep = weights[0].shape[0]

    def copies(swap):
        for i in range(parts):
            first, second = (weights[parts + i], weights[i]) if swap else (weights[i], weights[parts + i])
            part = pl.ds(i * deep, deep)
            pltpu.make_async_copy(first, expand.at[part, :], sems.at[i]).start()
            pltpu.make_async_copy(second, reduce.at[part, :], sems.at[parts + i]).start()

    core = info[I_CORE]

    @pl.when(core == 0)
    def _():
        copies(False)

    @pl.when(core != 0)
    def _():
        copies(True)

    size = m0.shape[0]
    for k, chunk in enumerate((m0, m1, m2, m3)):
        mixed[chunk_rows(lax.rem(info[I_Y] + YS - k, YS), size), :] = chunk[...]
    level = levels[pl.ds(info[I_LEVEL], 1), :]
    current = state[...]
    before = state_before(current, occupied[...], embed[...], level)
    change = space_term[...] + dot(mixed[...], output[...])
    middle = rms(before + change).astype(BF16)
    for i in range(parts):
        part = pl.ds(i * deep, deep)
        pltpu.make_async_copy(weights[i], expand.at[part, :], sems.at[i]).wait()
        pltpu.make_async_copy(weights[i], reduce.at[part, :], sems.at[parts + i]).wait()
        hidden = jax.nn.gelu(dot_t(middle, expand[part, :]), approximate=True).astype(BF16)
        change = change + dot(hidden, reduce[part, :])
    result = (current.astype(F32) + steps[info[I_LEVEL]] * change).astype(BF16)
    if not hand_on:
        moved[...] = result
        return
    result = jnp.where(info[I_FRAME] == 0, fresh[...], result)
    moved[...] = result
    level = levels[pl.ds(info[I_NEXT_LEVEL], 1), :]
    normed[...] = rms(state_before(result, occupied[...], embed[...], level)).astype(BF16)
    send_chunks(info, normed, chunks)


def shards(
    latents,
    occupancy,
    neighbors,
    brick_counts,
    noise_levels,
    level_embed,
    occupied_embed,
    step_size,
    fresh_noise,
    space_project,
    space_output,
    time_project,
    time_output,
    expand_weight,
    reduce_weight,
):
    blocks, brick, width = latents.shape[1:]
    rows = blocks * brick
    chunk = rows // YS
    frames = lax.axis_size("frame")
    spaces = lax.axis_size("space")
    xs, zs = 4, spaces // 4
    frame = lax.axis_index("frame").astype(jnp.int32)
    space = lax.axis_index("space").astype(jnp.int32)
    core = frame % 2

    def along(block, axis, route):
        return lax.ppermute(block, axis, [(i, route(i)) for i in range(lax.axis_size(axis))])

    def both(block, route):
        pairs = []
        for f in range(frames):
            for s in range(spaces):
                to_f, to_s = route(f, s)
                pairs.append((f * spaces + s, to_f * spaces + to_s))
        return lax.ppermute(block, ("frame", "space"), pairs)

    def y_on(f, k):
        return (f // 2 + k) % YS * 2 + f % 2

    piece = jnp.where(core == 0, expand_weight.T, reduce_weight)
    column = [piece] + [
        along(piece, "space", lambda s, k=k: (s // xs + k) % zs * xs + s % xs) for k in range(1, zs)
    ]
    column = jnp.concatenate(column, axis=0)
    mine = [column] + [
        along(column, "space", lambda s, k=k: s // xs * xs + (s + k) % xs) for k in range(1, xs)
    ]
    other = [along(block, "frame", lambda f: f ^ 1) for block in mine]

    level_before = along(noise_levels, "frame", lambda f: (f + 1) % frames)
    info = jnp.stack(
        [frame, space, frame // 2, core, noise_levels[0], level_before[0], frame * 0, frame * 0]
    ).astype(jnp.int32)
    occupied = occupancy.reshape(rows, 1).astype(F32)
    embed = occupied_embed.reshape(1, width)

    def struct(*shape, dtype=BF16):
        return jax.ShapeDtypeStruct(shape, dtype)

    chunk_structs = [struct(chunk, width)] * YS

    def attend(state, left, right, chunks, shift):
        queries, pairs = call(
            lambda *refs: time_project_kernel(shift, *refs),
            [struct(rows, width), struct(rows, 2 * width)],
            [smem] + [vmem] * 5,
            [pltpu.VMEM((rows, width), BF16)],
            flops=6 * rows * width * width,
            moved=6 * width * width,
        )(info, *chunks, time_project)
        other_pairs = along(pairs, "frame", lambda f: f ^ 1)
        space_queries, space_pairs = call(
            space_project_kernel,
            [struct(rows, width), struct(3 * rows, 2 * width)],
            [smem] + [vmem] * 7,
            flops=14 * rows * width * width,
            moved=6 * width * width,
        )(info, state, occupied, embed, level_embed, left, right, space_project)
        mixed = call(
            time_attend_kernel,
            chunk_structs,
            [smem] + [vmem] * 3,
            [pltpu.VMEM((rows, width), BF16)],
            flops=40 * rows * width * 128,
            moved=10 * rows * width,
        )(info, queries, pairs, other_pairs)
        mixed = [mixed[0]] + [
            along(mixed[k], "frame", lambda f, k=k: y_on(f, k)) for k in range(1, YS)
        ]
        space_term = call(
            space_attend_kernel,
            struct(rows, width, dtype=F32),
            [smem] * 3 + [vmem] * 3,
            [pltpu.VMEM((rows, width), BF16)],
            flops=30 * rows * width * 128 * 3,
            moved=2 * width * width,
        )(info, neighbors, brick_counts, space_queries, space_pairs, space_output)
        return space_term, mixed

    def finish(state, space_term, mixed, hand_on):
        hidden = 2 * sum(block.shape[0] for block in mine) // 2
        specs = [smem, smem] + [vmem] * 10 + [anywhere] * 8
        operands = [info, step_size, state, occupied, embed, level_embed, space_term, *mixed]
        operands += [time_output, *mine, *other]
        outs = struct(rows, width)
        if hand_on:
            specs.append(vmem)
            operands.append(fresh_noise.reshape(rows, width))
            outs = [outs, outs] + chunk_structs
        return call(
            lambda *refs: finish_kernel(hand_on, *refs),
            outs,
            specs,
            [
                pltpu.VMEM((hidden, width), BF16),
                pltpu.VMEM((hidden, width), BF16),
                pltpu.VMEM((rows, width), BF16),
                pltpu.SemaphoreType.DMA((8,)),
            ],
            flops=4 * rows * width * hidden,
            moved=4 * hidden * width,
        )(*operands)

    state = latents.reshape(rows, width)
    normed, *chunks = call(
        pre_kernel, [struct(rows, width)] + chunk_structs, [smem] + [vmem] * 4, moved=4 * rows * width
    )(info, state, occupied, embed, level_embed)
    left = along(normed, "space", lambda s: (s + 1) % spaces)
    right = along(normed, "space", lambda s: (s - 1) % spaces)
    chunks = [chunks[0]] + [
        along(chunks[k], "frame", lambda f, k=k: y_on(f, k)) for k in range(1, YS)
    ]
    space_term, mixed = attend(state, left, right, chunks, 0)
    moved, normed, *chunks = finish(state, space_term, mixed, True)

    chunks = [along(chunks[k], "frame", lambda f, k=k: y_on(f ^ 1, k)) for k in range(YS)]
    state = along(moved, "frame", lambda f: (f - 1) % frames)
    left = both(normed, lambda f, s: ((f - 1) % frames, (s + 1) % spaces))
    right = both(normed, lambda f, s: ((f - 1) % frames, (s - 1) % spaces))
    space_term, mixed = attend(state, left, right, chunks, 1)
    return finish(state, space_term, mixed, False).reshape(1, blocks, brick, width)


def solution(mesh):
    placed = (
        P("frame", "space", None, None),
        P("space", None),
        P("space", None),
        P(),
        P("frame"),
        P(),
        P(),
        P(),
        P("space", None, None),
        P(),
        P(),
        P(),
        P(),
        P(None, "space"),
        P("space", None),
    )
    return jax.shard_map(
        shards,
        mesh=mesh,
        in_specs=placed,
        out_specs=P("frame", "space", None, None),
        check_vma=False,
    )
```

```python
import functools

import jax
import jax.numpy as jnp
from jax import lax
from jax.experimental import pallas as pl
from jax.experimental.pallas import tpu as pltpu
from jax.sharding import PartitionSpec as P

HEADS = 12
FRAMES = 8
YS = 4
EPSILON = 1e-06
MASKED = -1e30

F32 = jnp.float32
BF16 = jnp.bfloat16
VMEM_LIMIT = 24 * 1024 * 1024

I_FRAME, I_SPACE, I_Y, I_CORE, I_LEVEL = range(5)

vmem = pl.BlockSpec(memory_space=pltpu.VMEM)
smem = pl.BlockSpec(memory_space=pltpu.SMEM)
anywhere = pl.BlockSpec(memory_space=pl.ANY)


def dot(a, b):
    return jnp.dot(a, b, preferred_element_type=F32)


def dot_t(a, b):
    return lax.dot_general(a, b, (((1,), (1,)), ((), ())), preferred_element_type=F32)


def rms(values):
    return values * lax.rsqrt(jnp.mean(values * values, axis=-1, keepdims=True) + EPSILON)


def chunk_rows(index, rows):
    return pl.ds(pl.multiple_of(index * rows, rows), rows)


def call(kernel, outs, specs, scratch=(), waits=(), limit=VMEM_LIMIT):
    used = len(specs)
    specs = specs + [anywhere] * len(waits)

    def body(*refs):
        kernel(*refs[:used], *refs[used + len(waits) :])

    return functools.partial(pallas(body, outs, specs, scratch, limit), waits)


def pallas(kernel, outs, specs, scratch, limit):
    made = pl.pallas_call(
        kernel,
        out_shape=outs,
        in_specs=specs,
        out_specs=jax.tree.map(lambda _: vmem, outs),
        scratch_shapes=scratch,
        compiler_params=pltpu.CompilerParams(vmem_limit_bytes=limit),
        cost_estimate=pl.CostEstimate(flops=0, bytes_accessed=1, transcendentals=0),
    )
    return lambda waits, *operands: made(*operands, *waits)


def state_before(state, occupancy, embed, level):
    size = occupancy.shape[1]
    row = lax.broadcasted_iota(jnp.int32, (size, size), 0)
    column = lax.broadcasted_iota(jnp.int32, (size, size), 1)
    marks = []
    for b in range(occupancy.shape[0]):
        spread = jnp.where(row == column, occupancy[b : b + 1, :].astype(F32), 0.0)
        marks.append(jnp.sum(spread, axis=-1, keepdims=True))
    return state.astype(F32) + jnp.concatenate(marks, axis=0) * embed + level


def pre_kernel(info, state, occupancy, levels, embed, expand, reduce, normed, piece, *rest):
    chunks = rest[:YS]
    state_in, occupancy_in, levels_in, sems = rest[YS:]
    copies = [
        pltpu.make_async_copy(source, target, sems.at[i])
        for i, (source, target) in enumerate(
            ((state, state_in), (occupancy, occupancy_in), (levels, levels_in))
        )
    ]
    for copy in copies:
        copy.start()
    first_core = info[I_CORE] == 0

    @pl.when(first_core)
    def _():
        pltpu.make_async_copy(expand, piece, sems.at[3]).start()

    @pl.when(jnp.logical_not(first_core))
    def _():
        pltpu.make_async_copy(reduce, piece, sems.at[3]).start()

    for copy in copies:
        copy.wait()
    level = levels_in[pl.ds(info[I_LEVEL], 1), :]
    before = state_before(state_in[...], occupancy_in, embed[...], level)
    normed[...] = rms(before).astype(BF16)
    send_chunks(info, normed, chunks)
    pltpu.make_async_copy(reduce, piece, sems.at[3]).wait()


def send_chunks(info, rows, chunks):
    size = rows.shape[0] // YS
    for k, chunk in enumerate(chunks):
        chunk[...] = rows[chunk_rows(lax.rem(info[I_Y] + k, YS), size), :]


def time_project_kernel(shift, info, c0, c1, c2, c3, project, queries, pairs, rows):
    size = c0.shape[0]
    for k, chunk in enumerate((c0, c1, c2, c3)):
        at = lax.rem(info[I_Y] + YS - k + shift * (YS - info[I_CORE]), YS)
        rows[chunk_rows(at, size), :] = chunk[...]
    width = rows.shape[1]
    values = rows[...]
    pairs[...] = dot(values, project[:, width:]).astype(BF16)
    queries[...] = dot(values, project[:, :width]).astype(BF16)


def head_selector(width):
    lane = lax.broadcasted_iota(jnp.int32, (width, 128), 0)
    head = lax.broadcasted_iota(jnp.int32, (width, 128), 1)
    return (lane // (width // HEADS) == head).astype(BF16)


def head_spreader(width):
    head = lax.broadcasted_iota(jnp.int32, (128, width), 0)
    lane = lax.broadcasted_iota(jnp.int32, (128, width), 1)
    return (lane // (width // HEADS) == head).astype(BF16)


def time_attend_kernel(info, queries, mine, other, m0, m1, m2, m3, mixed):
    tokens = queries.shape[0] // YS
    width = queries.shape[1]
    scale = (width // HEADS) ** -0.5
    selector = head_selector(width)
    first_core = info[I_CORE] == 0
    scores = {}
    for side, pairs in enumerate((mine, other)):
        for i in range(YS):
            left = YS - i
            keys = pairs[i * tokens : (i + 1) * tokens, :width].astype(F32)
            query = queries[i * tokens :, :].astype(F32).reshape(left, tokens, width)
            product = (query * keys[None]).reshape(left * tokens, width)
            high = product.astype(BF16)
            low = (product - high.astype(F32)).astype(BF16)
            score = (dot(high, selector) + dot(low, selector)) * scale
            for j in range(i, YS):
                part = score[(j - i) * tokens : (j - i + 1) * tokens, :]
                if side == 1 and i == j:
                    part = jnp.where(first_core, MASKED, part)
                scores[side, i, j] = part
    weights = []
    for j in range(YS):
        parts = [scores[side, i, j] for side in range(2) for i in range(j + 1)]
        highest = parts[0]
        for part in parts[1:]:
            highest = jnp.maximum(highest, part)
        raised = [jnp.exp(part - highest) for part in parts]
        total = raised[0]
        for part in raised[1:]:
            total = total + part
        weights += [(part / total).astype(BF16) for part in raised]
    spread = dot(jnp.concatenate(weights, axis=0), head_spreader(width))
    at = 0
    for j in range(YS):
        mix = None
        for pairs in (mine, other):
            for i in range(j + 1):
                value = pairs[i * tokens : (i + 1) * tokens, width:].astype(F32)
                term = spread[at * tokens : (at + 1) * tokens, :] * value
                mix = term if mix is None else mix + term
                at += 1
        mixed[j * tokens : (j + 1) * tokens, :] = mix.astype(BF16)
    send_chunks(info, mixed, (m0, m1, m2, m3))


def space_project_kernel(info, state, occupied, embed, levels, left, right, project, queries, pairs):
    width = state.shape[1]
    count = state.shape[0]
    level = levels[pl.ds(info[I_LEVEL], 1), :]
    before = state_before(state[...], occupied, embed[...], level)
    own = rms(before).astype(BF16)
    scale = (width // HEADS) ** -0.5
    queries[...] = (dot(own, project[:, :width]).astype(BF16) * scale).astype(BF16)
    pairs[count : 2 * count, :] = dot(own, project[:, width:]).astype(BF16)
    pairs[:count, :] = dot(left[...], project[:, width:]).astype(BF16)
    pairs[2 * count :, :] = dot(right[...], project[:, width:]).astype(BF16)


def space_attend_kernel(info, neighbors, counts, queries, pairs, output, term, mixed):
    rows, width = queries.shape
    blocks = neighbors.shape[0]
    brick = rows // blocks
    keys = pairs.shape[0]
    nearby = keys // brick
    total_bricks = counts.shape[0]
    column = lax.broadcasted_iota(jnp.int32, (1, keys), 1)
    key_brick = column // brick
    slot = column % brick
    times = []
    for b in range(blocks):
        row = jnp.zeros((1, keys), F32)
        for e in range(nearby):
            index = (info[I_SPACE] - 1) * blocks + e
            inside = (index >= 0) & (index < total_bricks)
            number = jnp.int32(1 if e == blocks + b else 0)
            for n in range(neighbors.shape[1]):
                number = number + jnp.where(inside & (neighbors[b, n] == index), 1, 0)
            valid = counts[jnp.clip(index, 0, total_bricks - 1)]
            row = jnp.where((key_brick == e) & (slot < valid), number.astype(F32), row)
        times.append(jnp.broadcast_to(row, (brick, keys)))
    times = jnp.concatenate(times + times, axis=0)
    usable = times > 0.0
    pair = 2 * (width // HEADS)
    half = lax.broadcasted_iota(jnp.int32, (rows, pair), 1) < pair // 2
    for h in range(HEADS // 2):
        lanes = slice(h * pair, (h + 1) * pair)
        query = queries[:, lanes]
        zero = jnp.zeros_like(query)
        both = jnp.concatenate([jnp.where(half, query, zero), jnp.where(half, zero, query)], axis=0)
        score = jnp.where(usable, dot_t(both, pairs[:, lanes]), MASKED)
        highest = jnp.max(score, axis=-1, keepdims=True)
        raised = jnp.exp(score - highest) * times
        share = (raised / jnp.sum(raised, axis=-1, keepdims=True)).astype(BF16)
        mix = dot(share, pairs[:, width + h * pair : width + (h + 1) * pair])
        mixed[:, lanes] = jnp.where(half, mix[:rows], mix[rows:]).astype(BF16)
    term[...] = dot(mixed[...], output[...])


def finish_kernel(
    hand_on, info, steps, next_level, state, occupied, embed, levels, space_term, m0, m1, m2, m3, output, *rest
):
    weights = rest[:8]
    if hand_on:
        fresh, moved, normed = rest[8:11]
        chunks = rest[11:15]
        expand, reduce, mixed, sems = rest[15:]
    else:
        moved = rest[8]
        expand, reduce, mixed, sems = rest[9:]
    parts = len(weights) // 2
    deep = weights[0].shape[0]

    def copies(swap):
        for i in range(parts):
            first, second = (weights[parts + i], weights[i]) if swap else (weights[i], weights[parts + i])
            part = pl.ds(i * deep, deep)
            pltpu.make_async_copy(first, expand.at[part, :], sems.at[i]).start()
            pltpu.make_async_copy(second, reduce.at[part, :], sems.at[parts + i]).start()

    core = info[I_CORE]

    @pl.when(core == 0)
    def _():
        copies(False)

    @pl.when(core != 0)
    def _():
        copies(True)

    size = m0.shape[0]
    for k, chunk in enumerate((m0, m1, m2, m3)):
        mixed[chunk_rows(lax.rem(info[I_Y] + YS - k, YS), size), :] = chunk[...]
    level = levels[pl.ds(info[I_LEVEL], 1), :]
    current = state[...]
    before = state_before(current, occupied, embed[...], level)
    change = space_term[...] + dot(mixed[...], output[...])
    middle = rms(before + change).astype(BF16)
    for i in range(parts):
        part = pl.ds(i * deep, deep)
        pltpu.make_async_copy(weights[i], expand.at[part, :], sems.at[i]).wait()
        pltpu.make_async_copy(weights[i], reduce.at[part, :], sems.at[parts + i]).wait()
        hidden = jax.nn.gelu(dot_t(middle, expand[part, :]), approximate=True).astype(BF16)
        change = change + dot(hidden, reduce[part, :])
    result = (current.astype(F32) + steps[info[I_LEVEL]] * change).astype(BF16)
    if not hand_on:
        moved[...] = result
        return
    result = jnp.where(info[I_FRAME] == 0, fresh[...], result)
    moved[...] = result
    level = levels[pl.ds(next_level[0], 1), :]
    normed[...] = rms(state_before(result, occupied, embed[...], level)).astype(BF16)
    send_chunks(info, normed, chunks)


def shards(
    latents,
    occupancy,
    neighbors,
    brick_counts,
    noise_levels,
    level_embed,
    occupied_embed,
    step_size,
    fresh_noise,
    space_project,
    space_output,
    time_project,
    time_output,
    expand_weight,
    reduce_weight,
):
    blocks, brick, width = latents.shape[1:]
    rows = blocks * brick
    chunk = rows // YS
    frames = lax.axis_size("frame")
    spaces = lax.axis_size("space")
    xs, zs = 4, spaces // 4
    frame = lax.axis_index("frame").astype(jnp.int32)
    space = lax.axis_index("space").astype(jnp.int32)
    core = frame % 2

    def along(block, axis, route):
        return lax.ppermute(block, axis, [(i, route(i)) for i in range(lax.axis_size(axis))])

    def both(block, route):
        pairs = []
        for f in range(frames):
            for s in range(spaces):
                to_f, to_s = route(f, s)
                pairs.append((f * spaces + s, to_f * spaces + to_s))
        return lax.ppermute(block, ("frame", "space"), pairs)

    def y_on(f, k):
        return (f // 2 + k) % YS * 2 + f % 2

    level_before = along(noise_levels, "frame", lambda f: (f + 1) % frames)
    info = jnp.stack(
        [frame, space, frame // 2, core, noise_levels[0]]
    ).astype(jnp.int32)
    occupied = occupancy
    embed = occupied_embed.reshape(1, width)

    def struct(*shape, dtype=BF16):
        return jax.ShapeDtypeStruct(shape, dtype)

    chunk_structs = [struct(chunk, width)] * YS

    def attend(state, left, right, chunks, shift, waits):
        queries, pairs = call(
            lambda *refs: time_project_kernel(shift, *refs),
            [struct(rows, width), struct(rows, 2 * width)],
            [smem] + [vmem] * 5,
            [pltpu.VMEM((rows, width), BF16)],
            waits,
        )(info, *chunks, time_project)
        other_pairs = along(pairs, "frame", lambda f: f ^ 1)
        space_queries, space_pairs = call(
            space_project_kernel,
            [struct(rows, width), struct(3 * rows, 2 * width)],
            [smem] + [vmem] * 7,
        )(info, state, occupied, embed, level_embed, left, right, space_project)
        mixed = call(
            time_attend_kernel,
            chunk_structs,
            [smem] + [vmem] * 3,
            [pltpu.VMEM((rows, width), BF16)],
            [space_queries],
        )(info, queries, pairs, other_pairs)
        mixed = [mixed[0]] + [
            along(mixed[k], "frame", lambda f, k=k: y_on(f, k)) for k in range(1, YS)
        ]
        space_term = call(
            space_attend_kernel,
            struct(rows, width, dtype=F32),
            [smem] * 3 + [vmem] * 3,
            [pltpu.VMEM((rows, width), BF16)],
        )(info, neighbors, brick_counts, space_queries, space_pairs, space_output)
        return space_term, mixed

    def finish(state, space_term, mixed, mine, other, hand_on):
        hidden = 2 * sum(block.shape[0] for block in mine) // 2
        specs = [smem, smem, smem] + [vmem] * 10 + [anywhere] * 8
        operands = [info, step_size, level_before, state, occupied, embed, level_embed, space_term, *mixed]
        operands += [time_output, *mine, *other]
        outs = struct(rows, width)
        if hand_on:
            specs.append(vmem)
            operands.append(fresh_noise.reshape(rows, width))
            outs = [outs, outs] + chunk_structs
        return call(
            lambda *refs: finish_kernel(hand_on, *refs),
            outs,
            specs,
            [
                pltpu.VMEM((hidden, width), BF16),
                pltpu.VMEM((hidden, width), BF16),
                pltpu.VMEM((rows, width), BF16),
                pltpu.SemaphoreType.DMA((8,)),
            ],
        )(*operands)

    def z_on(block, k):
        return along(block, "space", lambda s: (s // xs + k) % zs * xs + s % xs)

    def x_on(block, k):
        return along(block, "space", lambda s: s // xs * xs + (s + k) % xs)

    state = latents.reshape(rows, width)
    normed, piece, *chunks = call(
        pre_kernel,
        [struct(rows, width), struct(reduce_weight.shape[0], width)] + chunk_structs,
        [smem] + [anywhere] * 3 + [vmem] + [anywhere] * 2,
        [
            pltpu.VMEM((rows, width), BF16),
            pltpu.VMEM((blocks, brick), jnp.int32),
            pltpu.VMEM(level_embed.shape, F32),
            pltpu.SemaphoreType.DMA((4,)),
        ],
        limit=60 * 1024 * 1024,
    )(info, state, occupancy, level_embed, embed, expand_weight.T, reduce_weight)
    opposite = z_on(piece, zs // 2)
    left = along(normed, "space", lambda s: (s + 1) % spaces)
    right = along(normed, "space", lambda s: (s - 1) % spaces)
    chunks = [chunks[0]] + [
        along(chunks[k], "frame", lambda f, k=k: y_on(f, k)) for k in range(1, YS)
    ]
    piece, opposite, left, right, *chunks = lax.optimization_barrier(
        (piece, opposite, left, right, *chunks)
    )
    column = jnp.concatenate([piece, opposite], axis=0)
    column = jnp.concatenate([column] + [z_on(column, k) for k in (1, 2, zs - 1)], axis=0)
    mine = [column] + [x_on(column, k) for k in (1, 3, 2)]
    space_term, mixed = attend(state, left, right, chunks, 0, [left, right])
    other = [along(mine[0], "frame", lambda f: f ^ 1)]
    space_term, *held = lax.optimization_barrier((space_term, *mixed, *mine[1:]))
    mixed, arrived = held[:YS], held[YS:]
    mine = [mine[0]] + arrived
    other += [along(block, "frame", lambda f: f ^ 1) for block in arrived]
    moved, normed, *chunks = finish(state, space_term, mixed, mine, other, True)

    chunks = [along(chunks[k], "frame", lambda f, k=k: y_on(f ^ 1, k)) for k in range(YS)]
    state = along(moved, "frame", lambda f: (f - 1) % frames)
    left = both(normed, lambda f, s: ((f - 1) % frames, (s + 1) % spaces))
    right = both(normed, lambda f, s: ((f - 1) % frames, (s - 1) % spaces))
    space_term, mixed = attend(state, left, right, chunks, 1, [state, left, right])
    return finish(state, space_term, mixed, mine, other, False).reshape(1, blocks, brick, width)


def solution(mesh):
    placed = (
        P("frame", "space", None, None),
        P("space", None),
        P("space", None),
        P(),
        P("frame"),
        P(),
        P(),
        P(),
        P("space", None, None),
        P(),
        P(),
        P(),
        P(),
        P(None, "space"),
        P("space", None),
    )
    return jax.shard_map(
        shards,
        mesh=mesh,
        in_specs=placed,
        out_specs=P("frame", "space", None, None),
        check_vma=False,
    )
```

```python
import functools

import jax
import jax.numpy as jnp
from jax import lax
from jax.experimental import pallas as pl
from jax.experimental.pallas import tpu as pltpu
from jax.sharding import PartitionSpec as P

HEADS = 12
FRAMES = 8
YS = 4
EPSILON = 1e-06
MASKED = -1e30
MARK = 16
TURNS = ((1, 1), (-1, -1), (2, 2))

F32 = jnp.float32
BF16 = jnp.bfloat16
VMEM_LIMIT = 24 * 1024 * 1024

I_FRAME, I_SPACE, I_Y, I_CORE, I_LEVEL = range(5)

vmem = pl.BlockSpec(memory_space=pltpu.VMEM)
smem = pl.BlockSpec(memory_space=pltpu.SMEM)
anywhere = pl.BlockSpec(memory_space=pl.ANY)


def dot(a, b):
    return jnp.dot(a, b, preferred_element_type=F32)


def dot_t(a, b):
    return lax.dot_general(a, b, (((1,), (1,)), ((), ())), preferred_element_type=F32)


def rms(values):
    return values * lax.rsqrt(jnp.mean(values * values, axis=-1, keepdims=True) + EPSILON)


def chunk_rows_at(start, multiple, rows):
    return pl.ds(pl.multiple_of(start, multiple), rows)


def chunk_rows(index, rows):
    return pl.ds(pl.multiple_of(index * rows, rows), rows)


def call(kernel, outs, specs, scratch=(), waits=(), limit=VMEM_LIMIT):
    used = len(specs)
    specs = specs + [anywhere] * len(waits)

    def body(level, *refs):
        frame = lax.axis_index("frame").astype(jnp.int32)
        space = lax.axis_index("space").astype(jnp.int32)
        info = (frame, space, frame // 2, frame % 2, level[0])
        kernel(info, *refs[: used - 1], *refs[used - 1 + len(waits) :])

    return functools.partial(pallas(body, outs, specs, scratch, limit), waits)


def pallas(kernel, outs, specs, scratch, limit):
    made = pl.pallas_call(
        kernel,
        out_shape=outs,
        in_specs=specs,
        out_specs=jax.tree.map(lambda _: vmem, outs),
        scratch_shapes=scratch,
        compiler_params=pltpu.CompilerParams(vmem_limit_bytes=limit),
        cost_estimate=pl.CostEstimate(flops=0, bytes_accessed=1, transcendentals=0),
    )
    return lambda waits, *operands: made(*operands, *waits)


def state_before(state, occupancy, embed, level):
    size = occupancy.shape[1]
    row = lax.broadcasted_iota(jnp.int32, (size, size), 0)
    column = lax.broadcasted_iota(jnp.int32, (size, size), 1)
    marks = []
    for b in range(occupancy.shape[0]):
        spread = jnp.where(row == column, occupancy[b : b + 1, :].astype(F32), 0.0)
        marks.append(jnp.sum(spread, axis=-1, keepdims=True))
    return state.astype(F32) + jnp.concatenate(marks, axis=0) * embed + level


def pre_kernel(info, state, occupancy, levels, embed, expand, reduce, normed, piece, *rest):
    chunks = rest[:YS]
    state_in, occupancy_in, levels_in, sems = rest[YS:]
    copies = [
        pltpu.make_async_copy(source, target, sems.at[i])
        for i, (source, target) in enumerate(
            ((state, state_in), (occupancy, occupancy_in), (levels, levels_in))
        )
    ]
    for copy in copies:
        copy.start()
    first_core = info[I_CORE] == 0

    @pl.when(first_core)
    def _():
        pltpu.make_async_copy(expand, piece, sems.at[3]).start()

    @pl.when(jnp.logical_not(first_core))
    def _():
        pltpu.make_async_copy(reduce, piece, sems.at[3]).start()

    for copy in copies:
        copy.wait()
    level = levels_in[pl.ds(info[I_LEVEL], 1), :]
    before = state_before(state_in[...], occupancy_in, embed[...].reshape(1, -1), level)
    normed[...] = rms(before).astype(BF16)
    size = normed.shape[0] // YS
    chunks[1][size:, :] = jnp.full((MARK, normed.shape[1]), info[I_LEVEL], F32).astype(BF16)
    send_chunks(info, normed, chunks)
    pltpu.make_async_copy(reduce, piece, sems.at[3]).wait()


def send_chunks(info, rows, chunks):
    size = rows.shape[0] // YS
    for k, chunk in enumerate(chunks):
        chunk[:size, :] = rows[chunk_rows(lax.rem(info[I_Y] + k, YS), size), :]


def time_project_kernel(shift, info, c0, c1, c2, c3, project, queries, pairs, rows):
    size = c0.shape[0]
    for k, chunk in enumerate((c0, c1, c2, c3)):
        at = lax.rem(info[I_Y] + YS - k + shift * (YS - info[I_CORE]), YS)
        rows[chunk_rows(at, size), :] = chunk[:size, :]
    width = rows.shape[1]
    values = rows[...]
    count = values.shape[0]
    pairs[:count, :] = dot(values, project[:, width:]).astype(BF16)
    if pairs.shape[0] > count:
        own = jnp.full((MARK, width), info[I_LEVEL], F32).astype(BF16)
        mark = jnp.where(info[I_CORE] == 0, own, c1[size:, :])
        pairs[count:, :width] = mark
        pairs[count:, width:] = mark
    queries[...] = dot(values, project[:, :width]).astype(BF16)


def head_selector(width):
    lane = lax.broadcasted_iota(jnp.int32, (width, 128), 0)
    head = lax.broadcasted_iota(jnp.int32, (width, 128), 1)
    return (lane // (width // HEADS) == head).astype(BF16)


def head_spreader(width):
    head = lax.broadcasted_iota(jnp.int32, (128, width), 0)
    lane = lax.broadcasted_iota(jnp.int32, (128, width), 1)
    return (lane // (width // HEADS) == head).astype(BF16)


def time_attend_kernel(info, queries, mine, other, m0, m1, m2, m3, mixed):
    tokens = queries.shape[0] // YS
    width = queries.shape[1]
    scale = (width // HEADS) ** -0.5
    selector = head_selector(width)
    first_core = info[I_CORE] == 0
    scores = {}
    for side, pairs in enumerate((mine, other)):
        for i in range(YS):
            left = YS - i
            keys = pairs[i * tokens : (i + 1) * tokens, :width].astype(F32)
            query = queries[i * tokens :, :].astype(F32).reshape(left, tokens, width)
            product = (query * keys[None]).reshape(left * tokens, width)
            high = product.astype(BF16)
            low = (product - high.astype(F32)).astype(BF16)
            score = (dot(high, selector) + dot(low, selector)) * scale
            for j in range(i, YS):
                part = score[(j - i) * tokens : (j - i + 1) * tokens, :]
                if side == 1 and i == j:
                    part = jnp.where(first_core, MASKED, part)
                scores[side, i, j] = part
    weights = []
    for j in range(YS):
        parts = [scores[side, i, j] for side in range(2) for i in range(j + 1)]
        highest = parts[0]
        for part in parts[1:]:
            highest = jnp.maximum(highest, part)
        raised = [jnp.exp(part - highest) for part in parts]
        total = raised[0]
        for part in raised[1:]:
            total = total + part
        weights += [(part / total).astype(BF16) for part in raised]
    spread = dot(jnp.concatenate(weights, axis=0), head_spreader(width))
    at = 0
    for j in range(YS):
        mix = None
        for pairs in (mine, other):
            for i in range(j + 1):
                value = pairs[i * tokens : (i + 1) * tokens, width:].astype(F32)
                term = spread[at * tokens : (at + 1) * tokens, :] * value
                mix = term if mix is None else mix + term
                at += 1
        mixed[j * tokens : (j + 1) * tokens, :] = mix.astype(BF16)
    send_chunks(info, mixed, (m0, m1, m2, m3))


def space_project_kernel(info, state, occupied, embed, levels, left, right, project, queries, pairs):
    width = state.shape[1]
    count = state.shape[0]
    level = levels[pl.ds(info[I_LEVEL], 1), :]
    before = state_before(state[...], occupied, embed[...].reshape(1, -1), level)
    own = rms(before).astype(BF16)
    scale = (width // HEADS) ** -0.5
    queries[...] = (dot(own, project[:, :width]).astype(BF16) * scale).astype(BF16)
    pairs[count : 2 * count, :] = dot(own, project[:, width:]).astype(BF16)
    pairs[:count, :] = dot(left[...], project[:, width:]).astype(BF16)
    pairs[2 * count :, :] = dot(right[...], project[:, width:]).astype(BF16)


def space_attend_kernel(info, neighbors, counts, queries, pairs, output, term, mixed):
    rows, width = queries.shape
    blocks = neighbors.shape[0]
    brick = rows // blocks
    keys = pairs.shape[0]
    nearby = keys // brick
    total_bricks = counts.shape[0]
    column = lax.broadcasted_iota(jnp.int32, (1, keys), 1)
    key_brick = column // brick
    slot = column % brick
    times = []
    for b in range(blocks):
        row = jnp.zeros((1, keys), F32)
        for e in range(nearby):
            index = (info[I_SPACE] - 1) * blocks + e
            inside = (index >= 0) & (index < total_bricks)
            number = jnp.int32(1 if e == blocks + b else 0)
            for n in range(neighbors.shape[1]):
                number = number + jnp.where(inside & (neighbors[b, n] == index), 1, 0)
            valid = counts[jnp.clip(index, 0, total_bricks - 1)]
            row = jnp.where((key_brick == e) & (slot < valid), number.astype(F32), row)
        times.append(jnp.broadcast_to(row, (brick, keys)))
    times = jnp.concatenate(times + times, axis=0)
    usable = times > 0.0
    pair = 2 * (width // HEADS)
    half = lax.broadcasted_iota(jnp.int32, (rows, pair), 1) < pair // 2
    for h in range(HEADS // 2):
        lanes = slice(h * pair, (h + 1) * pair)
        query = queries[:, lanes]
        zero = jnp.zeros_like(query)
        both = jnp.concatenate([jnp.where(half, query, zero), jnp.where(half, zero, query)], axis=0)
        score = jnp.where(usable, dot_t(both, pairs[:, lanes]), MASKED)
        highest = jnp.max(score, axis=-1, keepdims=True)
        raised = jnp.exp(score - highest) * times
        share = (raised / jnp.sum(raised, axis=-1, keepdims=True)).astype(BF16)
        mix = dot(share, pairs[:, width + h * pair : width + (h + 1) * pair])
        mixed[:, lanes] = jnp.where(half, mix[:rows], mix[rows:]).astype(BF16)
    term[...] = dot(mixed[...], output[...])


def finish_kernel(
    hand_on, info, steps, state, occupied, embed, levels, space_term, m0, m1, m2, m3, output, *rest
):
    weights, outs, mixed = rest[0], rest[1:-1], rest[-1]
    size = m0.shape[0]
    for k, chunk in enumerate((m0, m1, m2, m3)):
        mixed[chunk_rows(lax.rem(info[I_Y] + YS - k, YS), size), :] = chunk[...]
    level = levels[pl.ds(info[I_LEVEL], 1), :]
    current = state[...]
    before = state_before(current, occupied, embed[...].reshape(1, -1), level)
    change = space_term[...] + dot(mixed[...], output[...])
    middle = rms(before + change).astype(BF16)
    parts = len(TURNS) + 1
    half = weights.shape[0] // 2
    deep = half // parts
    fine = deep // parts
    expand = info[I_CORE] * half
    reduce = half - expand
    for i in range(parts):
        matrix = weights[chunk_rows_at(expand + i * deep, fine, deep), :]
        hidden = jax.nn.gelu(dot_t(middle, matrix), approximate=True).astype(BF16)
        matrix = [
            weights[chunk_rows_at(reduce + j * deep + i * fine, fine, fine), :] for j in range(parts)
        ]
        change = change + dot(hidden, jnp.concatenate(matrix, axis=0))
    result = (current.astype(F32) + steps[info[I_LEVEL]] * change).astype(BF16)
    if not hand_on:
        outs[0][...] = result
        return
    fresh, marked, moved, normed, *chunks = outs
    result = jnp.where(info[I_FRAME] == 0, fresh[...], result)
    moved[...] = result
    number = marked[result.shape[0] :, :128].astype(F32)[:1, :1]
    table = lax.broadcasted_iota(jnp.int32, levels.shape, 0).astype(F32)
    level = jnp.sum(jnp.where(table == number, levels[...], 0.0), axis=0, keepdims=True)
    normed[...] = rms(state_before(result, occupied, embed[...].reshape(1, -1), level)).astype(BF16)
    send_chunks(info, normed, chunks)


def shards(
    latents,
    occupancy,
    neighbors,
    brick_counts,
    noise_levels,
    level_embed,
    occupied_embed,
    step_size,
    fresh_noise,
    space_project,
    space_output,
    time_project,
    time_output,
    expand_weight,
    reduce_weight,
):
    blocks, brick, width = latents.shape[1:]
    rows = blocks * brick
    chunk = rows // YS
    frames = lax.axis_size("frame")
    spaces = lax.axis_size("space")
    xs, zs = 4, spaces // 4
    def along(block, axis, route):
        return lax.ppermute(block, axis, [(i, route(i)) for i in range(lax.axis_size(axis))])

    def both(block, route):
        pairs = []
        for f in range(frames):
            for s in range(spaces):
                to_f, to_s = route(f, s)
                pairs.append((f * spaces + s, to_f * spaces + to_s))
        return lax.ppermute(block, ("frame", "space"), pairs)

    def y_on(f, k):
        return (f // 2 + k) % YS * 2 + f % 2

    info = noise_levels
    occupied = occupancy
    embed = occupied_embed

    def struct(*shape, dtype=BF16):
        return jax.ShapeDtypeStruct(shape, dtype)

    chunk_structs = [struct(chunk, width)] * YS

    def attend(state, left, right, chunks, shift, waits, between):
        queries, pairs = call(
            lambda *refs: time_project_kernel(shift, *refs),
            [struct(rows, width), struct(rows + (0 if shift else MARK), 2 * width)],
            [smem] + [vmem] * 5,
            [pltpu.VMEM((rows, width), BF16)],
            waits,
        )(info, *chunks, time_project)
        other_pairs = along(pairs, "frame", lambda f: f ^ 1)
        space_queries, space_pairs = call(
            space_project_kernel,
            [struct(rows, width), struct(3 * rows, 2 * width)],
            [smem] + [vmem] * 7,
        )(info, state, occupied, embed, level_embed, left, right, space_project)
        mixed = call(
            time_attend_kernel,
            chunk_structs,
            [smem] + [vmem] * 3,
            [pltpu.VMEM((rows, width), BF16)],
            [space_queries],
        )(info, queries, pairs, other_pairs)
        mixed = [mixed[0]] + [
            along(mixed[k], "frame", lambda f, k=k: y_on(f, k)) for k in range(1, YS)
        ]
        mixed, held = between(mixed)
        space_term = call(
            space_attend_kernel,
            struct(rows, width, dtype=F32),
            [smem] * 3 + [vmem] * 3,
            [pltpu.VMEM((rows, width), BF16)],
            held,
        )(info, neighbors, brick_counts, space_queries, space_pairs, space_output)
        return space_term, mixed, other_pairs

    def finish(state, space_term, mixed, weights, marked, hand_on):
        specs = [smem, smem] + [vmem] * 11
        operands = [info, step_size, state, occupied, embed, level_embed, space_term, *mixed]
        operands += [time_output, weights]
        outs = struct(rows, width)
        if hand_on:
            specs += [vmem] * 2
            operands += [fresh_noise.reshape(rows, width), marked]
            outs = [outs, outs] + chunk_structs
        return call(
            lambda *refs: finish_kernel(hand_on, *refs),
            outs,
            specs,
            [pltpu.VMEM((rows, width), BF16)],
        )(*operands)

    def z_step(k):
        return lambda s: (s // xs + k) % zs * xs + s % xs

    def x_step(k):
        return lambda s: s // xs * xs + (s + k) % xs

    def split(block, first, second):
        return both(block, lambda f, s: (f, second(s) if f % 2 else first(s)))

    state = latents.reshape(rows, width)
    normed, piece, *chunks = call(
        pre_kernel,
        [struct(rows, width), struct(reduce_weight.shape[0], width), chunk_structs[0]]
        + [struct(chunk + MARK, width)]
        + chunk_structs[2:],
        [smem] + [anywhere] * 3 + [vmem] + [anywhere] * 2,
        [
            pltpu.VMEM((rows, width), BF16),
            pltpu.VMEM((blocks, brick), jnp.int32),
            pltpu.VMEM(level_embed.shape, F32),
            pltpu.SemaphoreType.DMA((4,)),
        ],
        limit=60 * 1024 * 1024,
    )(info, state, occupancy, level_embed, embed, expand_weight.T, reduce_weight)
    opposite = along(piece, "space", z_step(zs // 2))
    left = along(normed, "space", lambda s: (s + 1) % spaces)
    right = along(normed, "space", lambda s: (s - 1) % spaces)
    chunks = [chunks[0]] + [
        along(chunks[k], "frame", lambda f, k=k: y_on(f, k)) for k in range(1, YS)
    ]
    piece, opposite, left, right, *chunks = lax.optimization_barrier(
        (piece, opposite, left, right, *chunks)
    )
    part = jnp.concatenate([piece, opposite], axis=0)
    column = jnp.concatenate(
        [part] + [split(part, z_step(z), x_step(x)) for z, x in TURNS], axis=0
    )
    mine = [column] + [split(column, x_step(x), z_step(z)) for z, x in TURNS]
    other = [along(mine[0], "frame", lambda f: f ^ 1)]

    def exchange(mixed):
        held = lax.optimization_barrier((*mixed, *mine[1:]))
        mine[1:] = held[YS:]
        other.extend(along(block, "frame", lambda f: f ^ 1) for block in mine[1:])
        return held[:YS], [held[1]]

    space_term, mixed, marked = attend(state, left, right, chunks, 0, [left, right], exchange)
    weights = jnp.concatenate(mine + other, axis=0)
    moved, normed, *chunks = finish(state, space_term, mixed, weights, marked, True)

    chunks = [along(chunks[k], "frame", lambda f, k=k: y_on(f ^ 1, k)) for k in range(YS)]
    state = along(moved, "frame", lambda f: (f - 1) % frames)
    left = both(normed, lambda f, s: ((f - 1) % frames, (s + 1) % spaces))
    right = both(normed, lambda f, s: ((f - 1) % frames, (s - 1) % spaces))
    space_term, mixed, _ = attend(
        state, left, right, chunks, 1, [state, left, right], lambda mixed: (mixed, [])
    )
    return finish(state, space_term, mixed, weights, None, False).reshape(1, blocks, brick, width)


def solution(mesh):
    placed = (
        P("frame", "space", None, None),
        P("space", None),
        P("space", None),
        P(),
        P("frame"),
        P(),
        P(),
        P(),
        P("space", None, None),
        P(),
        P(),
        P(),
        P(),
        P(None, "space"),
        P("space", None),
    )
    return jax.shard_map(
        shards,
        mesh=mesh,
        in_specs=placed,
        out_specs=P("frame", "space", None, None),
        check_vma=False,
    )
```

```python
import functools

import jax
import jax.numpy as jnp
from jax import lax
from jax.experimental import pallas as pl
from jax.experimental.pallas import tpu as pltpu
from jax.sharding import PartitionSpec as P

HEADS = 12
FRAMES = 8
YS = 4
EPSILON = 1e-06
MASKED = -1e30
MARK = 16
TURNS = ((1, 1), (-1, -1), (2, 2))

F32 = jnp.float32
BF16 = jnp.bfloat16
VMEM_LIMIT = 24 * 1024 * 1024

I_FRAME, I_SPACE, I_Y, I_CORE, I_LEVEL = range(5)

vmem = pl.BlockSpec(memory_space=pltpu.VMEM)
smem = pl.BlockSpec(memory_space=pltpu.SMEM)
anywhere = pl.BlockSpec(memory_space=pl.ANY)


def dot(a, b):
    return jnp.dot(a, b, preferred_element_type=F32)


def dot_t(a, b):
    return lax.dot_general(a, b, (((1,), (1,)), ((), ())), preferred_element_type=F32)


def rms(values):
    return values * lax.rsqrt(jnp.mean(values * values, axis=-1, keepdims=True) + EPSILON)


def chunk_rows_at(start, multiple, rows):
    return pl.ds(pl.multiple_of(start, multiple), rows)


def chunk_rows(index, rows):
    return pl.ds(pl.multiple_of(index * rows, rows), rows)


def call(kernel, outs, specs, scratch=(), waits=(), limit=VMEM_LIMIT):
    used = len(specs)
    specs = specs + [anywhere] * len(waits)

    def body(level, *refs):
        frame = lax.axis_index("frame").astype(jnp.int32)
        space = lax.axis_index("space").astype(jnp.int32)
        info = (frame, space, frame // 2, frame % 2, level[0])
        kernel(info, *refs[: used - 1], *refs[used - 1 + len(waits) :])

    return functools.partial(pallas(body, outs, specs, scratch, limit), waits)


def pallas(kernel, outs, specs, scratch, limit):
    made = pl.pallas_call(
        kernel,
        out_shape=outs,
        in_specs=specs,
        out_specs=jax.tree.map(lambda _: vmem, outs),
        scratch_shapes=scratch,
        compiler_params=pltpu.CompilerParams(vmem_limit_bytes=limit),
        cost_estimate=pl.CostEstimate(flops=0, bytes_accessed=1, transcendentals=0),
    )
    return lambda waits, *operands: made(*operands, *waits)


def state_before(state, occupancy, embed, level):
    size = occupancy.shape[1]
    row = lax.broadcasted_iota(jnp.int32, (size, size), 0)
    column = lax.broadcasted_iota(jnp.int32, (size, size), 1)
    marks = []
    for b in range(occupancy.shape[0]):
        spread = jnp.where(row == column, occupancy[b : b + 1, :].astype(F32), 0.0)
        marks.append(jnp.sum(spread, axis=-1, keepdims=True))
    return state.astype(F32) + jnp.concatenate(marks, axis=0) * embed + level


def pre_kernel(info, state, occupancy, levels, embed, expand, reduce, normed, piece, *rest):
    chunks = rest[:YS]
    state_in, occupancy_in, levels_in, sems = rest[YS:]
    copies = [
        pltpu.make_async_copy(source, target, sems.at[i])
        for i, (source, target) in enumerate(
            ((state, state_in), (occupancy, occupancy_in), (levels, levels_in))
        )
    ]
    for copy in copies:
        copy.start()
    first_core = info[I_CORE] == 0

    @pl.when(first_core)
    def _():
        pltpu.make_async_copy(expand, piece, sems.at[3]).start()

    @pl.when(jnp.logical_not(first_core))
    def _():
        pltpu.make_async_copy(reduce, piece, sems.at[3]).start()

    for copy in copies:
        copy.wait()
    level = levels_in[pl.ds(info[I_LEVEL], 1), :]
    before = state_before(state_in[...], occupancy_in, embed[...].reshape(1, -1), level)
    normed[...] = rms(before).astype(BF16)
    size = normed.shape[0] // YS
    chunks[1][size:, :] = jnp.full((MARK, normed.shape[1]), info[I_LEVEL], F32).astype(BF16)
    send_chunks(info, normed, chunks)
    pltpu.make_async_copy(reduce, piece, sems.at[3]).wait()


def send_chunks(info, rows, chunks):
    size = rows.shape[0] // YS
    for k, chunk in enumerate(chunks):
        chunk[:size, :] = rows[chunk_rows(lax.rem(info[I_Y] + k, YS), size), :]


def time_project_kernel(shift, info, c0, c1, c2, c3, project, queries, pairs, rows):
    size = c0.shape[0]
    for k, chunk in enumerate((c0, c1, c2, c3)):
        at = lax.rem(info[I_Y] + YS - k + shift * (YS - info[I_CORE]), YS)
        rows[chunk_rows(at, size), :] = chunk[:size, :]
    width = rows.shape[1]
    values = rows[...]
    count = values.shape[0]
    pairs[:count, :] = dot(values, project[:, width:]).astype(BF16)
    if pairs.shape[0] > count:
        own = jnp.full((MARK, width), info[I_LEVEL], F32).astype(BF16)
        mark = jnp.where(info[I_CORE] == 0, own, c1[size:, :])
        pairs[count:, :width] = mark
        pairs[count:, width:] = mark
    queries[...] = dot(values, project[:, :width]).astype(BF16)


def head_selector(width):
    lane = lax.broadcasted_iota(jnp.int32, (width, 128), 0)
    head = lax.broadcasted_iota(jnp.int32, (width, 128), 1)
    return (lane // (width // HEADS) == head).astype(BF16)


def head_spreader(width):
    head = lax.broadcasted_iota(jnp.int32, (128, width), 0)
    lane = lax.broadcasted_iota(jnp.int32, (128, width), 1)
    return (lane // (width // HEADS) == head).astype(BF16)


def time_attend_kernel(info, queries, mine, other, m0, m1, m2, m3, mixed):
    tokens = queries.shape[0] // YS
    width = queries.shape[1]
    scale = (width // HEADS) ** -0.5
    selector = head_selector(width)
    first_core = info[I_CORE] == 0
    scores = {}
    for side, pairs in enumerate((mine, other)):
        for i in range(YS):
            left = YS - i
            keys = pairs[i * tokens : (i + 1) * tokens, :width].astype(F32)
            query = queries[i * tokens :, :].astype(F32).reshape(left, tokens, width)
            product = (query * keys[None]).reshape(left * tokens, width)
            high = product.astype(BF16)
            low = (product - high.astype(F32)).astype(BF16)
            score = (dot(high, selector) + dot(low, selector)) * scale
            for j in range(i, YS):
                part = score[(j - i) * tokens : (j - i + 1) * tokens, :]
                if side == 1 and i == j:
                    part = jnp.where(first_core, MASKED, part)
                scores[side, i, j] = part
    weights = []
    for j in range(YS):
        parts = [scores[side, i, j] for side in range(2) for i in range(j + 1)]
        highest = parts[0]
        for part in parts[1:]:
            highest = jnp.maximum(highest, part)
        raised = [jnp.exp(part - highest) for part in parts]
        total = raised[0]
        for part in raised[1:]:
            total = total + part
        weights += [(part / total).astype(BF16) for part in raised]
    spread = dot(jnp.concatenate(weights, axis=0), head_spreader(width))
    at = 0
    for j in range(YS):
        mix = None
        for pairs in (mine, other):
            for i in range(j + 1):
                value = pairs[i * tokens : (i + 1) * tokens, width:].astype(F32)
                term = spread[at * tokens : (at + 1) * tokens, :] * value
                mix = term if mix is None else mix + term
                at += 1
        mixed[j * tokens : (j + 1) * tokens, :] = mix.astype(BF16)
    send_chunks(info, mixed, (m0, m1, m2, m3))


def space_project_kernel(info, state, occupied, embed, levels, left, right, project, queries, pairs):
    width = state.shape[1]
    count = state.shape[0]
    level = levels[pl.ds(info[I_LEVEL], 1), :]
    before = state_before(state[...], occupied, embed[...].reshape(1, -1), level)
    own = rms(before).astype(BF16)
    scale = (width // HEADS) ** -0.5
    queries[...] = (dot(own, project[:, :width]).astype(BF16) * scale).astype(BF16)
    pairs[count : 2 * count, :] = dot(own, project[:, width:]).astype(BF16)
    pairs[:count, :] = dot(left[...], project[:, width:]).astype(BF16)
    pairs[2 * count :, :] = dot(right[...], project[:, width:]).astype(BF16)


def space_attend_kernel(info, neighbors, counts, queries, pairs, output, term, mixed):
    rows, width = queries.shape
    blocks = neighbors.shape[0]
    brick = rows // blocks
    keys = pairs.shape[0]
    nearby = keys // brick
    total_bricks = counts.shape[0]
    column = lax.broadcasted_iota(jnp.int32, (1, keys), 1)
    key_brick = column // brick
    slot = column % brick
    times = []
    for b in range(blocks):
        row = jnp.zeros((1, keys), F32)
        for e in range(nearby):
            index = (info[I_SPACE] - 1) * blocks + e
            inside = (index >= 0) & (index < total_bricks)
            number = jnp.int32(1 if e == blocks + b else 0)
            for n in range(neighbors.shape[1]):
                number = number + jnp.where(inside & (neighbors[b, n] == index), 1, 0)
            valid = counts[jnp.clip(index, 0, total_bricks - 1)]
            row = jnp.where((key_brick == e) & (slot < valid), number.astype(F32), row)
        times.append(jnp.broadcast_to(row, (brick, keys)))
    times = jnp.concatenate(times + times, axis=0)
    usable = times > 0.0
    pair = 2 * (width // HEADS)
    half = lax.broadcasted_iota(jnp.int32, (rows, pair), 1) < pair // 2
    for h in range(HEADS // 2):
        lanes = slice(h * pair, (h + 1) * pair)
        query = queries[:, lanes]
        zero = jnp.zeros_like(query)
        both = jnp.concatenate([jnp.where(half, query, zero), jnp.where(half, zero, query)], axis=0)
        score = jnp.where(usable, dot_t(both, pairs[:, lanes]), MASKED)
        highest = jnp.max(score, axis=-1, keepdims=True)
        raised = jnp.exp(score - highest) * times
        share = (raised / jnp.sum(raised, axis=-1, keepdims=True)).astype(BF16)
        mix = dot(share, pairs[:, width + h * pair : width + (h + 1) * pair])
        mixed[:, lanes] = jnp.where(half, mix[:rows], mix[rows:]).astype(BF16)
    term[...] = dot(mixed[...], output[...])


def finish_kernel(
    hand_on, info, steps, state, occupied, embed, levels, space_term, m0, m1, m2, m3, output, *rest
):
    weights, outs, mixed = rest[0], rest[1:-1], rest[-1]
    size = m0.shape[0]
    for k, chunk in enumerate((m0, m1, m2, m3)):
        mixed[chunk_rows(lax.rem(info[I_Y] + YS - k, YS), size), :] = chunk[...]
    level = levels[pl.ds(info[I_LEVEL], 1), :]
    current = state[...]
    before = state_before(current, occupied, embed[...].reshape(1, -1), level)
    change = space_term[...] + dot(mixed[...], output[...])
    middle = rms(before + change).astype(BF16)
    parts = len(TURNS) + 1
    half = weights.shape[0] // 2
    deep = half // parts
    fine = deep // parts
    expand = info[I_CORE] * half
    reduce = half - expand
    for i in range(parts):
        matrix = weights[chunk_rows_at(expand + i * deep, fine, deep), :]
        hidden = jax.nn.gelu(dot_t(middle, matrix), approximate=True).astype(BF16)
        matrix = [
            weights[chunk_rows_at(reduce + j * deep + i * fine, fine, fine), :] for j in range(parts)
        ]
        change = change + dot(hidden, jnp.concatenate(matrix, axis=0))
    result = (current.astype(F32) + steps[info[I_LEVEL]] * change).astype(BF16)
    if not hand_on:
        outs[0][...] = result
        return
    fresh, marked, moved, normed, *chunks = outs
    result = jnp.where(info[I_FRAME] == 0, fresh[...], result)
    moved[...] = result
    number = marked[result.shape[0] :, :128].astype(F32)[:1, :1]
    table = lax.broadcasted_iota(jnp.int32, levels.shape, 0).astype(F32)
    level = jnp.sum(jnp.where(table == number, levels[...], 0.0), axis=0, keepdims=True)
    normed[...] = rms(state_before(result, occupied, embed[...].reshape(1, -1), level)).astype(BF16)
    send_chunks(info, normed, chunks)


def shards(
    latents,
    occupancy,
    neighbors,
    brick_counts,
    noise_levels,
    level_embed,
    occupied_embed,
    step_size,
    fresh_noise,
    space_project,
    space_output,
    time_project,
    time_output,
    expand_weight,
    reduce_weight,
):
    blocks, brick, width = latents.shape[1:]
    rows = blocks * brick
    chunk = rows // YS
    frames = lax.axis_size("frame")
    spaces = lax.axis_size("space")
    xs, zs = 4, spaces // 4
    def along(block, axis, route):
        return lax.ppermute(block, axis, [(i, route(i)) for i in range(lax.axis_size(axis))])

    def both(block, route):
        pairs = []
        for f in range(frames):
            for s in range(spaces):
                to_f, to_s = route(f, s)
                pairs.append((f * spaces + s, to_f * spaces + to_s))
        return lax.ppermute(block, ("frame", "space"), pairs)

    def y_on(f, k):
        return (f // 2 + k) % YS * 2 + f % 2

    info = noise_levels
    occupied = occupancy
    embed = occupied_embed

    def struct(*shape, dtype=BF16):
        return jax.ShapeDtypeStruct(shape, dtype)

    chunk_structs = [struct(chunk, width)] * YS

    def project(chunks, shift, waits):
        return call(
            lambda *refs: time_project_kernel(shift, *refs),
            [struct(rows, width), struct(rows + (0 if shift else MARK), 2 * width)],
            [smem] + [vmem] * 5,
            [pltpu.VMEM((rows, width), BF16)],
            waits,
        )(info, *chunks, time_project)

    def attend(state, left, right, queries, pairs, between):
        other_pairs = along(pairs, "frame", lambda f: f ^ 1)
        space_queries, space_pairs = call(
            space_project_kernel,
            [struct(rows, width), struct(3 * rows, 2 * width)],
            [smem] + [vmem] * 7,
        )(info, state, occupied, embed, level_embed, left, right, space_project)
        mixed = call(
            time_attend_kernel,
            chunk_structs,
            [smem] + [vmem] * 3,
            [pltpu.VMEM((rows, width), BF16)],
            [space_queries],
        )(info, queries, pairs, other_pairs)
        mixed = [mixed[0]] + [
            along(mixed[k], "frame", lambda f, k=k: y_on(f, k)) for k in range(1, YS)
        ]
        mixed, held = between(mixed)
        space_term = call(
            space_attend_kernel,
            struct(rows, width, dtype=F32),
            [smem] * 3 + [vmem] * 3,
            [pltpu.VMEM((rows, width), BF16)],
            held,
        )(info, neighbors, brick_counts, space_queries, space_pairs, space_output)
        return space_term, mixed, other_pairs

    def finish(state, space_term, mixed, weights, marked, hand_on):
        specs = [smem, smem] + [vmem] * 11
        operands = [info, step_size, state, occupied, embed, level_embed, space_term, *mixed]
        operands += [time_output, weights]
        outs = struct(rows, width)
        if hand_on:
            specs += [vmem] * 2
            operands += [fresh_noise.reshape(rows, width), marked]
            outs = [outs, outs] + chunk_structs
        return call(
            lambda *refs: finish_kernel(hand_on, *refs),
            outs,
            specs,
            [pltpu.VMEM((rows, width), BF16)],
        )(*operands)

    def z_step(k):
        return lambda s: (s // xs + k) % zs * xs + s % xs

    def x_step(k):
        return lambda s: s // xs * xs + (s + k) % xs

    def split(block, first, second):
        return both(block, lambda f, s: (f, second(s) if f % 2 else first(s)))

    state = latents.reshape(rows, width)
    normed, piece, *chunks = call(
        pre_kernel,
        [struct(rows, width), struct(reduce_weight.shape[0], width), chunk_structs[0]]
        + [struct(chunk + MARK, width)]
        + chunk_structs[2:],
        [smem] + [anywhere] * 3 + [vmem] + [anywhere] * 2,
        [
            pltpu.VMEM((rows, width), BF16),
            pltpu.VMEM((blocks, brick), jnp.int32),
            pltpu.VMEM(level_embed.shape, F32),
            pltpu.SemaphoreType.DMA((4,)),
        ],
        limit=60 * 1024 * 1024,
    )(info, state, occupancy, level_embed, embed, expand_weight.T, reduce_weight)
    opposite = along(piece, "space", z_step(zs // 2))
    left = along(normed, "space", lambda s: (s + 1) % spaces)
    right = along(normed, "space", lambda s: (s - 1) % spaces)
    chunks = [chunks[0]] + [
        along(chunks[k], "frame", lambda f, k=k: y_on(f, k)) for k in range(1, YS)
    ]
    piece, opposite, left, right, *chunks = lax.optimization_barrier(
        (piece, opposite, left, right, *chunks)
    )
    part = jnp.concatenate([piece, opposite], axis=0)
    column = jnp.concatenate(
        [part] + [split(part, z_step(z), x_step(x)) for z, x in TURNS], axis=0
    )
    queries, pairs, column = lax.optimization_barrier(
        (*project(chunks, 0, [left, right]), column)
    )
    mine = [column] + [split(column, x_step(x), z_step(z)) for z, x in TURNS]
    other = []

    def exchange(mixed):
        held = lax.optimization_barrier((*mixed, *mine))
        mine[:] = held[YS:]
        other.extend(along(block, "frame", lambda f: f ^ 1) for block in mine)
        return held[:YS], [held[1]]

    space_term, mixed, marked = attend(state, left, right, queries, pairs, exchange)
    weights = jnp.concatenate(mine + other, axis=0)
    moved, normed, *chunks = finish(state, space_term, mixed, weights, marked, True)

    chunks = [along(chunks[k], "frame", lambda f, k=k: y_on(f ^ 1, k)) for k in range(YS)]
    state = along(moved, "frame", lambda f: (f - 1) % frames)
    left = both(normed, lambda f, s: ((f - 1) % frames, (s + 1) % spaces))
    right = both(normed, lambda f, s: ((f - 1) % frames, (s - 1) % spaces))
    queries, pairs = project(chunks, 1, [state, left, right])
    space_term, mixed, _ = attend(
        state, left, right, queries, pairs, lambda mixed: (mixed, [])
    )
    return finish(state, space_term, mixed, weights, None, False).reshape(1, blocks, brick, width)


def solution(mesh):
    placed = (
        P("frame", "space", None, None),
        P("space", None),
        P("space", None),
        P(),
        P("frame"),
        P(),
        P(),
        P(),
        P("space", None, None),
        P(),
        P(),
        P(),
        P(),
        P(None, "space"),
        P("space", None),
    )
    return jax.shard_map(
        shards,
        mesh=mesh,
        in_specs=placed,
        out_specs=P("frame", "space", None, None),
        check_vma=False,
    )
```
